128 devices in a mesh: section: 16 (over x_hi, z, core), dp: 8 (over y, x_lo).
Axes of the slice: x: 4 (x_hi: 2, x_lo: 2; x = x_hi * 2 + x_lo), y: 4, z: 4, core: 2. Of those that a mesh axis runs over, the one named last changes fastest.
Arguments:
- layer_input: bfloat16 [16, 1024, 8192], P('section', 'dp'), may hold values from -6 to 6
- top_grad: bfloat16 [1024, 8192], P('dp'), may hold values from -6 to 6
- mean: float32 [16, 2, 8192, 128], P('section', None, 'dp'), may hold values from -6 to 6
- hessian: float32 [16, 2, 8192, 128], P('section', None, 'dp'), may hold values from 1 to 10
- momentum: float32 [16, 2, 8192, 128], P('section', None, 'dp'), may hold values from -4 to 4
- noise: bfloat16 [16, 8, 2, 8192, 128], P('section', None, None, 'dp'), may hold values from -5 to 5
- noise_next: bfloat16 [16, 8, 2, 8192, 128], P('section', None, None, 'dp'), may hold values from -5 to 5
Outputs:
- input_grad: bfloat16 [16, 1024, 8192], P('section', 'dp')
- new_mean: float32 [16, 2, 8192, 128], P('section', None, 'dp')
- new_hessian: float32 [16, 2, 8192, 128], P('section', None, 'dp')
- new_momentum: float32 [16, 2, 8192, 128], P('section', None, 'dp')
- next_weights: bfloat16 [16, 8, 2, 8192, 128], P('section', None, None, 'dp')
The draws below stay inside these ranges and needn't reach their ends.
All inputs are finite; a program needn't handle non-finite values.
Results may differ from the reference program's by a relative error of at most 0.024.
Values may be sent and summed in bfloat16 or wider, within the bound.
A program may use at most 128 MiB of HBM per device.

```python
import math
import jax
import jax.numpy as jnp
from jax import lax

D = 8192
BOTTLENECK = 128
TOK_DEV = 128
TOKENS = 1024
N_SECTION = 16
N_DP = 8


def steps_of(own_key, dims, cuts, least, high):
    factor_of = 1.0
    for position, blocks in cuts:
        heights = jax.random.uniform(jax.random.fold_in(jax.random.fold_in(own_key, 6), position), (blocks,), jnp.float32, least / len(cuts), high / len(cuts))
        factor_of = factor_of * jnp.repeat(jnp.exp(heights), dims[position] // blocks).reshape((-1,) + (1,) * (len(dims) - 1 - position))
    return factor_of


def centred(stream_key, dims, scale, reach, cuts=(), dtype=jnp.bfloat16):
    drawn = scale * jax.random.normal(stream_key, dims, jnp.float32)
    if cuts:
        drawn = drawn * steps_of(stream_key, dims, cuts, -0.22, 0.18)
    return jnp.clip(drawn, -reach, reach).astype(dtype)


def setup_inputs(seed: int = 0) -> dict:
    key_of = jax.random.split(jax.random.key(seed), 8)
    layer_input = centred(key_of[0], (N_SECTION, TOKENS, D), 1.0, 6.0, ((0, 16), (1, 8)))
    top_grad = centred(key_of[1], (TOKENS, D), 1.0, 6.0, ((0, 8),))
    mean = centred(key_of[2], (N_SECTION, 2, D, BOTTLENECK), 1.0, 6.0, ((0, 16), (2, 8)), jnp.float32)
    hessian = jnp.clip(jnp.exp(math.log(10.0) - 2.3025851 * jax.random.uniform(key_of[3], (N_SECTION, 2, D, BOTTLENECK), jnp.float32) ** steps_of(key_of[3], (N_SECTION, 2, D, BOTTLENECK), ((0, 16), (2, 8)), -0.2, 0.2)), 1.0, 10.0)
    momentum = centred(key_of[4], (N_SECTION, 2, D, BOTTLENECK), 0.3, 4.0, ((0, 16), (2, 8)), jnp.float32)
    noise = centred(key_of[5], (N_SECTION, N_DP, 2, D, BOTTLENECK), 1.0, 5.0, ((0, 16), (3, 8)))
    noise_next = centred(key_of[6], (N_SECTION, N_DP, 2, D, BOTTLENECK), 1.0, 5.0, ((0, 16), (3, 8)))
    return dict(layer_input=layer_input, top_grad=top_grad, mean=mean, hessian=hessian, momentum=momentum, noise=noise, noise_next=noise_next)


sample_size = 4.0
weight_decay = 0.05
first_decay = 0.9
second_decay = 0.9
step_rate = 0.5
branch_gain = 0.5
step_number = 10.0

def silu_slope(values):
    logistic = jax.nn.sigmoid(values)
    return logistic * (1.0 + values * (1.0 - logistic))

def rounded(values):
    return lax.optimization_barrier(values.astype(jnp.bfloat16)).astype(jnp.float32)

def reference(layer_input, top_grad, mean, hessian, momentum, noise, noise_next):
    in_scale = 1.0 / math.sqrt(D)
    out_scale = branch_gain / math.sqrt(BOTTLENECK)
    incoming = top_grad.reshape(N_DP, TOK_DEV, D)
    grad_list = []
    mean_list = []
    hessian_list = []
    momentum_list = []
    weight_list = []
    for section_index in range(N_SECTION - 1, -1, -1):
        precision_root = jnp.sqrt(sample_size * (hessian[section_index] + weight_decay))
        spread = 1.0 / precision_root
        drawn_noise = noise[section_index].astype(jnp.float32)
        weights = rounded(mean[section_index][None] + spread[None] * drawn_noise)
        weight_in = weights[:, 0]
        weight_out = weights[:, 1]
        layer_rows = layer_input[section_index].reshape(N_DP, TOK_DEV, D).astype(jnp.float32)
        preact = jnp.einsum('ntd,ndr->ntr', layer_rows, weight_in) * in_scale
        hidden = rounded(jax.nn.silu(preact))
        incoming_f = incoming.astype(jnp.float32)
        back_hidden = jnp.einsum('ntd,ndr->ntr', incoming_f, weight_out) * out_scale
        branch = rounded(back_hidden * silu_slope(preact))
        out_grad = (incoming_f + jnp.einsum('ntr,ndr->ntd', branch, weight_in) * in_scale).astype(jnp.bfloat16)
        grad_in = jnp.einsum('ntd,ntr->ndr', layer_rows, branch) * in_scale
        grad_out = jnp.einsum('ntd,ntr->ndr', incoming_f, hidden) * out_scale
        pieces = rounded(jnp.stack([grad_in, grad_out], 1))
        grad_mean = lax.optimization_barrier(jnp.mean(pieces, 0))
        hess_est = lax.optimization_barrier(jnp.mean(pieces * drawn_noise, 0)) * precision_root
        own_hessian = hessian[section_index]
        own_mean = mean[section_index]
        new_momentum = first_decay * momentum[section_index] + (1.0 - first_decay) * grad_mean
        new_hessian = second_decay * own_hessian + (1.0 - second_decay) * hess_est + 0.5 * (1.0 - second_decay) ** 2 * (own_hessian - hess_est) ** 2 / (own_hessian + weight_decay)
        new_mean = own_mean - step_rate * (new_momentum / (1.0 - first_decay ** step_number) + weight_decay * own_mean) / (new_hessian + weight_decay)
        next_spread = 1.0 / jnp.sqrt(sample_size * (new_hessian + weight_decay))
        next_weights = (new_mean[None] + next_spread[None] * noise_next[section_index].astype(jnp.float32)).astype(jnp.bfloat16)
        grad_list = [out_grad.reshape(TOKENS, D)] + grad_list
        mean_list = [new_mean] + mean_list
        hessian_list = [new_hessian] + hessian_list
        momentum_list = [new_momentum] + momentum_list
        weight_list = [next_weights] + weight_list
        incoming = out_grad
    return (jnp.stack(grad_list), jnp.stack(mean_list), jnp.stack(hessian_list), jnp.stack(momentum_list), jnp.stack(weight_list))
```

```python
import functools
import math

import jax
import jax.numpy as jnp
from jax import lax
from jax.experimental import pallas as pl
from jax.experimental.pallas import tpu as pltpu
from jax.sharding import PartitionSpec as P

MESH = pl.DeviceIdType.MESH
F32 = jnp.float32
BF16 = jnp.bfloat16

sample_size = 4.0
weight_decay = 0.05
first_decay = 0.9
second_decay = 0.9
step_rate = 0.5
branch_gain = 0.5
step_number = 10.0

CHUNK = 16
PIECES = 4


def chain_kernel(
    n_sec, n_dp,
    rows_hbm, top_hbm, mean_hbm, hess_hbm, noise_hbm,
    ig_hbm, rows_t, inc_t, branch_t, hidden_t,
    mean_v, spread_v, noise_v, rows_v, inc_v, out_v, send_w, w_v, preact_v, slope_v, hidden_v, branch_v,
    state_sem, noise_sem, rows_sem, top_sem, local_sem,
    w_send, w_recv, rt_send, rt_recv, it_send, it_recv, h_send, h_recv, b_send, b_recv, c_send, c_recv,
):
    s = lax.axis_index("section")
    j = lax.axis_index("dp")
    last = n_sec - 1
    tokens = rows_v.shape[1]
    width = rows_v.shape[2]
    n_chunks = tokens // CHUNK
    per = n_dp // PIECES
    in_scale = 1.0 / math.sqrt(width * n_dp)
    out_scale = branch_gain / math.sqrt(branch_v.shape[1])

    def peer_of(k):
        return lax.rem(j + k, n_dp)

    def source_of(k):
        return lax.rem(j + n_dp - k, n_dp)

    def remote(src, dst, send, recv, **device):
        return pltpu.make_async_remote_copy(
            src_ref=src, dst_ref=dst, send_sem=send, recv_sem=recv, device_id=device, device_id_type=MESH
        )

    mean_in = pltpu.make_async_copy(mean_hbm, mean_v, state_sem.at[0])
    hess_in = pltpu.make_async_copy(hess_hbm, spread_v, state_sem.at[1])
    hess_in.start()
    mean_in.start()
    for k in range(1, n_dp + 1):
        pltpu.make_async_copy(noise_hbm.at[peer_of(k)], noise_v.at[k - 1], noise_sem.at[k - 1]).start()
    for b in range(n_dp):
        pltpu.make_async_copy(rows_hbm.at[:, pl.ds(b * width, width)], rows_v.at[b], rows_sem.at[b]).start()

    def top_copy(b):
        return pltpu.make_async_copy(top_hbm.at[:, pl.ds(b * width, width)], inc_v.at[b], top_sem.at[b])

    @pl.when(s == last)
    def _():
        for b in range(n_dp):
            top_copy(b).start()

    barrier = pltpu.get_barrier_semaphore()
    for k in range(1, n_dp):
        pl.semaphore_signal(barrier, inc=1, device_id={"dp": peer_of(k)}, device_id_type=MESH)
    above = lax.rem(s + 1, n_sec)
    below = lax.rem(s + n_sec - 1, n_sec)
    pl.semaphore_signal(barrier, inc=1, device_id={"section": above}, device_id_type=MESH)
    pl.semaphore_signal(barrier, inc=1, device_id={"section": below}, device_id_type=MESH)

    hess_in.wait()
    mean_in.wait()
    step_rows = min(128, width)

    def each_rows(body):
        for i in range(2):
            def turn(r, carry):
                body(i, pl.ds(pl.multiple_of(r * step_rows, step_rows), step_rows))
                return carry
            lax.fori_loop(0, width // step_rows, turn, 0)

    def make_spread(i, rr):
        spread_v[i, rr, :] = 1.0 / jnp.sqrt(sample_size * (spread_v[i, rr, :] + weight_decay))

    each_rows(make_spread)
    pl.semaphore_wait(barrier, n_dp + 1)

    def weight_copy(k):
        return remote(send_w.at[k - 1], w_v.at[j], w_send.at[k - 1], w_recv.at[k - 1], dp=peer_of(k))

    def make_weights(k, carry):
        pltpu.make_async_copy(noise_hbm.at[peer_of(k)], noise_v.at[k - 1], noise_sem.at[k - 1]).wait()

        def body(i, rr):
            send_w[k - 1, i, rr, :] = (
                mean_v[i, rr, :] + spread_v[i, rr, :] * noise_v[k - 1, i, rr, :].astype(F32)
            ).astype(BF16)

        each_rows(body)
        weight_copy(k).start()
        return carry

    lax.fori_loop(1, n_dp, make_weights, 0)
    pltpu.make_async_copy(noise_hbm.at[j], noise_v.at[n_dp - 1], noise_sem.at[n_dp - 1]).wait()

    def own_weights(i, rr):
        w_v[j, i, rr, :] = (
            mean_v[i, rr, :] + spread_v[i, rr, :] * noise_v[n_dp - 1, i, rr, :].astype(F32)
        ).astype(BF16)

    each_rows(own_weights)
    for b in range(n_dp):
        pltpu.make_async_copy(rows_hbm.at[:, pl.ds(b * width, width)], rows_v.at[b], rows_sem.at[b]).wait()

    preact_v[...] = jnp.dot(rows_v[j], w_v[j, 0], preferred_element_type=F32)

    def add_preact(k, carry):
        src = source_of(k)
        weight_copy(k).wait_recv()
        preact_v[...] += jnp.dot(rows_v[src], w_v[src, 0], preferred_element_type=F32)
        return carry

    lax.fori_loop(1, n_dp, add_preact, 0)
    preact = preact_v[...] * in_scale
    gate = jax.nn.sigmoid(preact)
    hidden_v[...] = (preact * gate).astype(BF16)
    slope_v[...] = gate * (1.0 + preact * (1.0 - gate)) * out_scale

    @pl.when(s == last)
    def _():
        for b in range(n_dp):
            top_copy(b).wait()

    def chain_copy(c, p):
        part = (pl.ds(p * per, per), pl.ds(pl.multiple_of(c * CHUNK, CHUNK), CHUNK))
        return remote(out_v.at[part], inc_v.at[part], c_send.at[c, p], c_recv.at[c, p], section=below)

    def inc_copy(c, k):
        tok = pl.ds(pl.multiple_of(c * CHUNK, CHUNK), CHUNK)
        return remote(inc_v.at[peer_of(k), tok], inc_t.at[j, tok], it_send.at[k - 1], it_recv.at[k - 1], dp=peer_of(k))

    def rows_copy(k):
        return remote(rows_v.at[peer_of(k)], rows_t.at[j], rt_send.at[k - 1], rt_recv.at[k - 1], dp=peer_of(k))

    def hidden_copy(k):
        return remote(hidden_v, hidden_t.at[j], h_send.at[k - 1], h_recv.at[k - 1], dp=peer_of(k))

    def branch_copy(k):
        return remote(branch_v, branch_t.at[j], b_send.at[k - 1], b_recv.at[k - 1], dp=peer_of(k))

    def chunk_turn(c, carry):
        tok = pl.ds(pl.multiple_of(c * CHUNK, CHUNK), CHUNK)
        back = jnp.zeros((CHUNK, branch_v.shape[1]), F32)
        for p in range(PIECES):
            @pl.when(s < last)
            def _():
                chain_copy(c, p).wait_recv()
            for b in range(p * per, (p + 1) * per):
                back += jnp.dot(inc_v[b, tok, :], w_v[b, 1], preferred_element_type=F32)
        branch = (back * slope_v[tok, :]).astype(BF16)
        branch_v[tok, :] = branch
        for p in range(PIECES):
            for b in range(p * per, (p + 1) * per):
                through = lax.dot_general(
                    branch, w_v[b, 0], (((1,), (1,)), ((), ())), preferred_element_type=F32
                )
                out_v[b, tok, :] = (inc_v[b, tok, :].astype(F32) + through * in_scale).astype(BF16)

            @pl.when(s > 0)
            def _():
                chain_copy(c, p).start()
        def send_inc(k, carry):
            inc_copy(c, k).start()
            return carry
        lax.fori_loop(1, n_dp, send_inc, 0)

        @pl.when(c == 0)
        def _():
            def send_rows(k, carry):
                rows_copy(k).start()
                hidden_copy(k).start()
                return carry
            lax.fori_loop(1, n_dp, send_rows, 0)
        return carry

    lax.fori_loop(0, n_chunks, chunk_turn, 0)

    own = [
        pltpu.make_async_copy(branch_v, branch_t.at[j], local_sem.at[0]),
        pltpu.make_async_copy(hidden_v, hidden_t.at[j], local_sem.at[1]),
        pltpu.make_async_copy(rows_v.at[j], rows_t.at[j], local_sem.at[2]),
        pltpu.make_async_copy(inc_v.at[j], inc_t.at[j], local_sem.at[3]),
    ] + [
        pltpu.make_async_copy(out_v.at[b], ig_hbm.at[:, pl.ds(b * width, width)], local_sem.at[4 + b])
        for b in range(n_dp)
    ]
    def send_branch(k, carry):
        branch_copy(k).start()
        return carry
    lax.fori_loop(1, n_dp, send_branch, 0)
    for copy in own:
        copy.start()

    def finish(k, carry):
        weight_copy(k).wait_send()
        rows_copy(k).wait()
        hidden_copy(k).wait()
        branch_copy(k).wait()
        whole = remote(inc_v.at[peer_of(k)], inc_t.at[j], it_send.at[k - 1], it_recv.at[k - 1], dp=peer_of(k))
        whole.wait()
        return carry

    lax.fori_loop(1, n_dp, finish, 0)

    @pl.when(s > 0)
    def _():
        def sent(c, carry):
            for p in range(PIECES):
                chain_copy(c, p).wait_send()
            return carry
        lax.fori_loop(0, n_chunks, sent, 0)

    for copy in own:
        copy.wait()


def chain(n_sec, n_dp, rows, top, mean, hess, noise):
    tokens, depth = rows.shape
    width = depth // n_dp
    rank = mean.shape[-1]
    n_chunks = tokens // CHUNK
    dma = pltpu.SemaphoreType.DMA
    hbm = pl.BlockSpec(memory_space=pl.ANY)
    return pl.pallas_call(
        functools.partial(chain_kernel, n_sec, n_dp),
        out_shape=(
            jax.ShapeDtypeStruct((tokens, depth), BF16),
            jax.ShapeDtypeStruct((n_dp, tokens, width), BF16),
            jax.ShapeDtypeStruct((n_dp, tokens, width), BF16),
            jax.ShapeDtypeStruct((n_dp, tokens, rank), BF16),
            jax.ShapeDtypeStruct((n_dp, tokens, rank), BF16),
        ),
        in_specs=[hbm] * 5,
        out_specs=(hbm,) * 5,
        scratch_shapes=[
            pltpu.VMEM((2, width, rank), F32),
            pltpu.VMEM((2, width, rank), F32),
            pltpu.VMEM((n_dp, 2, width, rank), BF16),
            pltpu.VMEM((n_dp, tokens, width), BF16),
            pltpu.VMEM((n_dp, tokens, width), BF16),
            pltpu.VMEM((n_dp, tokens, width), BF16),
            pltpu.VMEM((n_dp - 1, 2, width, rank), BF16),
            pltpu.VMEM((n_dp, 2, width, rank), BF16),
            pltpu.VMEM((tokens, rank), F32),
            pltpu.VMEM((tokens, rank), F32),
            pltpu.VMEM((tokens, rank), BF16),
            pltpu.VMEM((tokens, rank), BF16),
            dma((2,)), dma((n_dp,)), dma((n_dp,)), dma((n_dp,)), dma((4 + n_dp,)),
        ]
        + [dma((n_dp - 1,))] * 10
        + [dma((n_chunks, PIECES))] * 2,
        compiler_params=pltpu.CompilerParams(
            collective_id=0, has_side_effects=True, vmem_limit_bytes=48 * 1024 * 1024
        ),
        cost_estimate=pl.CostEstimate(flops=10 * tokens * depth * rank, bytes_accessed=20 * 2**20, transcendentals=0),
    )(rows, top, mean, hess, noise)


def update_kernel(
    in_scale, out_scale, n_dp,
    rows_t, inc_t, branch_t, hidden_t, mean_r, hess_r, mom_r, noise_r, next_r,
    mean_o, hess_o, mom_o, weights_o,
):
    contract = (((0,), (0,)), ((), ()))
    for i in range(2):
        total = None
        for d in range(n_dp):
            if i == 0:
                grad = lax.dot_general(rows_t[d], branch_t[d], contract, preferred_element_type=F32) * in_scale
            else:
                grad = lax.dot_general(inc_t[d], hidden_t[d], contract, preferred_element_type=F32) * out_scale
            grad = grad.astype(BF16).astype(F32)
            with_noise = grad * noise_r[d, i].astype(F32)
            if total is None:
                total, total_noise = grad, with_noise
            else:
                total, total_noise = total + grad, total_noise + with_noise
        own_hessian = hess_r[i]
        own_mean = mean_r[i]
        grad_mean = total * (1.0 / n_dp)
        hess_est = total_noise * (1.0 / n_dp) * jnp.sqrt(sample_size * (own_hessian + weight_decay))
        new_momentum = first_decay * mom_r[i] + (1.0 - first_decay) * grad_mean
        new_hessian = (
            second_decay * own_hessian
            + (1.0 - second_decay) * hess_est
            + 0.5 * (1.0 - second_decay) ** 2 * (own_hessian - hess_est) ** 2 / (own_hessian + weight_decay)
        )
        new_mean = own_mean - step_rate * (
            new_momentum / (1.0 - first_decay**step_number) + weight_decay * own_mean
        ) / (new_hessian + weight_decay)
        next_spread = 1.0 / jnp.sqrt(sample_size * (new_hessian + weight_decay))
        mean_o[i] = new_mean
        hess_o[i] = new_hessian
        mom_o[i] = new_momentum
        for d in range(n_dp):
            weights_o[d, i] = (new_mean + next_spread * next_r[d, i].astype(F32)).astype(BF16)


def update(n_dp, depth, rows_t, inc_t, branch_t, hidden_t, mean, hess, mom, noise, noise_next):
    _, tokens, width = rows_t.shape
    rank = mean.shape[-1]
    block = 128
    in_scale = 1.0 / math.sqrt(depth)
    out_scale = branch_gain / math.sqrt(rank)
    cols = pl.BlockSpec((n_dp, tokens, block), lambda r: (0, 0, r))
    small = pl.BlockSpec((n_dp, tokens, rank), lambda r: (0, 0, 0))
    state = pl.BlockSpec((2, block, rank), lambda r: (0, r, 0))
    wide = pl.BlockSpec((n_dp, 2, block, rank), lambda r: (0, 0, r, 0))
    shape = jax.ShapeDtypeStruct(mean.shape, F32)
    return pl.pallas_call(
        functools.partial(update_kernel, in_scale, out_scale, n_dp),
        grid=(width // block,),
        out_shape=(shape, shape, shape, jax.ShapeDtypeStruct(noise.shape, BF16)),
        in_specs=[cols, cols, small, small, state, state, state, wide, wide],
        out_specs=(state, state, state, wide),
        compiler_params=pltpu.CompilerParams(vmem_limit_bytes=40 * 1024 * 1024),
        cost_estimate=pl.CostEstimate(
            flops=4 * n_dp * tokens * width * rank, bytes_accessed=22 * 2**20, transcendentals=0
        ),
    )(rows_t, inc_t, branch_t, hidden_t, mean, hess, mom, noise, noise_next)


def on_device(n_sec, n_dp, layer_input, top_grad, mean, hessian, momentum, noise, noise_next):
    input_grad, rows_t, inc_t, branch_t, hidden_t = chain(
        n_sec, n_dp, layer_input[0], top_grad, mean[0], hessian[0], noise[0]
    )
    new_mean, new_hessian, new_momentum, next_weights = update(
        n_dp, layer_input.shape[-1], rows_t, inc_t, branch_t, hidden_t,
        mean[0], hessian[0], momentum[0], noise[0], noise_next[0],
    )
    return (input_grad[None], new_mean[None], new_hessian[None], new_momentum[None], next_weights[None])


def solution(mesh):
    in_specs = (
        P("section", "dp", None),
        P("dp", None),
        P("section", None, "dp", None),
        P("section", None, "dp", None),
        P("section", None, "dp", None),
        P("section", None, None, "dp", None),
        P("section", None, None, "dp", None),
    )
    out_specs = (
        P("section", "dp", None),
        P("section", None, "dp", None),
        P("section", None, "dp", None),
        P("section", None, "dp", None),
        P("section", None, None, "dp", None),
    )
    return jax.shard_map(
        functools.partial(on_device, mesh.shape["section"], mesh.shape["dp"]),
        mesh=mesh, in_specs=in_specs, out_specs=out_specs, check_vma=False,
    )
```

```python
import functools
import math

import jax
import jax.numpy as jnp
from jax import lax
from jax.experimental import pallas as pl
from jax.experimental.pallas import tpu as pltpu
from jax.sharding import PartitionSpec as P

MESH = pl.DeviceIdType.MESH
F32 = jnp.float32
BF16 = jnp.bfloat16

sample_size = 4.0
weight_decay = 0.05
first_decay = 0.9
second_decay = 0.9
step_rate = 0.5
branch_gain = 0.5
step_number = 10.0

CHUNK = 16
PIECES = 4


def chain_kernel(
    n_sec, n_dp,
    rows_hbm, top_hbm, mean_hbm, hess_hbm, noise_hbm,
    ig_hbm, rows_t, inc_t, branch_t, hidden_t,
    mean_v, spread_v, noise_v, rows_v, inc_v, out_v, send_w, w_v, preact_v, slope_v, hidden_v, branch_v,
    state_sem, noise_sem, rows_sem, top_sem, local_sem,
    w_send, w_recv, rt_send, rt_recv, it_send, it_recv, h_send, h_recv, b_send, b_recv, c_send, c_recv,
):
    s = lax.axis_index("section")
    j = lax.axis_index("dp")
    last = n_sec - 1
    tokens = rows_v.shape[1]
    width = rows_v.shape[2]
    n_chunks = tokens // CHUNK
    per = n_dp // PIECES
    in_scale = 1.0 / math.sqrt(width * n_dp)
    out_scale = branch_gain / math.sqrt(branch_v.shape[1])

    def peer_of(k):
        return lax.rem(j + k, n_dp)

    def source_of(k):
        return lax.rem(j + n_dp - k, n_dp)

    def remote(src, dst, send, recv, **device):
        return pltpu.make_async_remote_copy(
            src_ref=src, dst_ref=dst, send_sem=send, recv_sem=recv, device_id=device, device_id_type=MESH
        )

    mean_in = pltpu.make_async_copy(mean_hbm, mean_v, state_sem.at[0])
    hess_in = pltpu.make_async_copy(hess_hbm, spread_v, state_sem.at[1])
    hess_in.start()
    mean_in.start()
    for k in range(1, n_dp + 1):
        pltpu.make_async_copy(noise_hbm.at[peer_of(k)], noise_v.at[k - 1], noise_sem.at[k - 1]).start()
    for b in range(n_dp):
        pltpu.make_async_copy(rows_hbm.at[:, pl.ds(b * width, width)], rows_v.at[b], rows_sem.at[b]).start()

    def top_copy(b):
        return pltpu.make_async_copy(top_hbm.at[:, pl.ds(b * width, width)], inc_v.at[b], top_sem.at[b])

    @pl.when(s == last)
    def _():
        for b in range(n_dp):
            top_copy(b).start()

    barrier = pltpu.get_barrier_semaphore()
    for k in range(1, n_dp):
        pl.semaphore_signal(barrier, inc=1, device_id={"dp": peer_of(k)}, device_id_type=MESH)
    above = lax.rem(s + 1, n_sec)
    below = lax.rem(s + n_sec - 1, n_sec)
    pl.semaphore_signal(barrier, inc=1, device_id={"section": above}, device_id_type=MESH)
    pl.semaphore_signal(barrier, inc=1, device_id={"section": below}, device_id_type=MESH)

    hess_in.wait()
    mean_in.wait()
    step_rows = min(128, width)

    def each_rows(body):
        for i in range(2):
            def turn(r, carry):
                body(i, pl.ds(pl.multiple_of(r * step_rows, step_rows), step_rows))
                return carry
            lax.fori_loop(0, width // step_rows, turn, 0)

    def make_spread(i, rr):
        spread_v[i, rr, :] = 1.0 / jnp.sqrt(sample_size * (spread_v[i, rr, :] + weight_decay))

    each_rows(make_spread)
    pl.semaphore_wait(barrier, n_dp + 1)

    def weight_copy(k):
        return remote(send_w.at[k - 1], w_v.at[j], w_send.at[k - 1], w_recv.at[k - 1], dp=peer_of(k))

    def make_weights(k, carry):
        pltpu.make_async_copy(noise_hbm.at[peer_of(k)], noise_v.at[k - 1], noise_sem.at[k - 1]).wait()

        def body(i, rr):
            send_w[k - 1, i, rr, :] = (
                mean_v[i, rr, :] + spread_v[i, rr, :] * noise_v[k - 1, i, rr, :].astype(F32)
            ).astype(BF16)

        each_rows(body)
        weight_copy(k).start()
        return carry

    lax.fori_loop(1, n_dp, make_weights, 0)
    pltpu.make_async_copy(noise_hbm.at[j], noise_v.at[n_dp - 1], noise_sem.at[n_dp - 1]).wait()

    def own_weights(i, rr):
        w_v[j, i, rr, :] = (
            mean_v[i, rr, :] + spread_v[i, rr, :] * noise_v[n_dp - 1, i, rr, :].astype(F32)
        ).astype(BF16)

    each_rows(own_weights)
    for b in range(n_dp):
        pltpu.make_async_copy(rows_hbm.at[:, pl.ds(b * width, width)], rows_v.at[b], rows_sem.at[b]).wait()

    preact_v[...] = jnp.dot(rows_v[j], w_v[j, 0], preferred_element_type=F32)

    def add_preact(k, carry):
        src = source_of(k)
        weight_copy(k).wait_recv()
        preact_v[...] += jnp.dot(rows_v[src], w_v[src, 0], preferred_element_type=F32)
        return carry

    lax.fori_loop(1, n_dp, add_preact, 0)
    preact = preact_v[...] * in_scale
    gate = jax.nn.sigmoid(preact)
    hidden_v[...] = (preact * gate).astype(BF16)
    slope_v[...] = gate * (1.0 + preact * (1.0 - gate)) * out_scale

    @pl.when(s == last)
    def _():
        for b in range(n_dp):
            top_copy(b).wait()

    def chain_copy(c, p):
        part = (pl.ds(p * per, per), pl.ds(pl.multiple_of(c * CHUNK, CHUNK), CHUNK))
        return remote(out_v.at[part], inc_v.at[part], c_send.at[c, p], c_recv.at[c, p], section=below)

    def inc_copy(c, k):
        tok = pl.ds(pl.multiple_of(c * CHUNK, CHUNK), CHUNK)
        return remote(inc_v.at[peer_of(k), tok], inc_t.at[j, tok], it_send.at[k - 1], it_recv.at[k - 1], dp=peer_of(k))

    def rows_copy(k):
        return remote(rows_v.at[peer_of(k)], rows_t.at[j], rt_send.at[k - 1], rt_recv.at[k - 1], dp=peer_of(k))

    def hidden_copy(k):
        return remote(hidden_v, hidden_t.at[j], h_send.at[k - 1], h_recv.at[k - 1], dp=peer_of(k))

    def branch_copy(k):
        return remote(branch_v, branch_t.at[j], b_send.at[k - 1], b_recv.at[k - 1], dp=peer_of(k))

    late = jnp.logical_and(s >= n_sec // 2, s < n_sec // 2 + 2)

    def send_inc(c):
        def turn(k, carry):
            inc_copy(c, k).start()
            return carry
        lax.fori_loop(1, n_dp, turn, 0)

    def chunk_turn(c, carry):
        tok = pl.ds(pl.multiple_of(c * CHUNK, CHUNK), CHUNK)
        back = jnp.zeros((CHUNK, branch_v.shape[1]), F32)
        for p in range(PIECES):
            @pl.when(s < last)
            def _():
                chain_copy(c, p).wait_recv()
            for b in range(p * per, (p + 1) * per):
                back += jnp.dot(inc_v[b, tok, :], w_v[b, 1], preferred_element_type=F32)
        branch = (back * slope_v[tok, :]).astype(BF16)
        branch_v[tok, :] = branch
        for p in range(PIECES):
            for b in range(p * per, (p + 1) * per):
                through = lax.dot_general(
                    branch, w_v[b, 0], (((1,), (1,)), ((), ())), preferred_element_type=F32
                )
                out_v[b, tok, :] = (inc_v[b, tok, :].astype(F32) + through * in_scale).astype(BF16)

            @pl.when(s > 0)
            def _():
                chain_copy(c, p).start()

        @pl.when(jnp.logical_not(late))
        def _():
            send_inc(c)

        return carry

    def send_rows(k, carry):
        rows_copy(k).start()
        hidden_copy(k).start()
        return carry

    lax.fori_loop(1, n_dp, send_rows, 0)
    lax.fori_loop(0, n_chunks, chunk_turn, 0)

    @pl.when(late)
    def _():
        def send_late(c, carry):
            send_inc(c)
            return carry
        lax.fori_loop(0, n_chunks, send_late, 0)

    own = [
        pltpu.make_async_copy(branch_v, branch_t.at[j], local_sem.at[0]),
        pltpu.make_async_copy(hidden_v, hidden_t.at[j], local_sem.at[1]),
        pltpu.make_async_copy(rows_v.at[j], rows_t.at[j], local_sem.at[2]),
        pltpu.make_async_copy(inc_v.at[j], inc_t.at[j], local_sem.at[3]),
    ] + [
        pltpu.make_async_copy(out_v.at[b], ig_hbm.at[:, pl.ds(b * width, width)], local_sem.at[4 + b])
        for b in range(n_dp)
    ]
    def send_branch(k, carry):
        branch_copy(k).start()
        return carry
    lax.fori_loop(1, n_dp, send_branch, 0)
    for copy in own:
        copy.start()

    def finish(k, carry):
        weight_copy(k).wait_send()
        rows_copy(k).wait()
        hidden_copy(k).wait()
        branch_copy(k).wait()
        whole = remote(inc_v.at[peer_of(k)], inc_t.at[j], it_send.at[k - 1], it_recv.at[k - 1], dp=peer_of(k))
        whole.wait()
        return carry

    lax.fori_loop(1, n_dp, finish, 0)

    @pl.when(s > 0)
    def _():
        def sent(c, carry):
            for p in range(PIECES):
                chain_copy(c, p).wait_send()
            return carry
        lax.fori_loop(0, n_chunks, sent, 0)

    for copy in own:
        copy.wait()


def chain(n_sec, n_dp, rows, top, mean, hess, noise):
    tokens, depth = rows.shape
    width = depth // n_dp
    rank = mean.shape[-1]
    n_chunks = tokens // CHUNK
    dma = pltpu.SemaphoreType.DMA
    hbm = pl.BlockSpec(memory_space=pl.ANY)
    return pl.pallas_call(
        functools.partial(chain_kernel, n_sec, n_dp),
        out_shape=(
            jax.ShapeDtypeStruct((tokens, depth), BF16),
            jax.ShapeDtypeStruct((n_dp, tokens, width), BF16),
            jax.ShapeDtypeStruct((n_dp, tokens, width), BF16),
            jax.ShapeDtypeStruct((n_dp, tokens, rank), BF16),
            jax.ShapeDtypeStruct((n_dp, tokens, rank), BF16),
        ),
        in_specs=[hbm] * 5,
        out_specs=(hbm,) * 5,
        scratch_shapes=[
            pltpu.VMEM((2, width, rank), F32),
            pltpu.VMEM((2, width, rank), F32),
            pltpu.VMEM((n_dp, 2, width, rank), BF16),
            pltpu.VMEM((n_dp, tokens, width), BF16),
            pltpu.VMEM((n_dp, tokens, width), BF16),
            pltpu.VMEM((n_dp, tokens, width), BF16),
            pltpu.VMEM((n_dp - 1, 2, width, rank), BF16),
            pltpu.VMEM((n_dp, 2, width, rank), BF16),
            pltpu.VMEM((tokens, rank), F32),
            pltpu.VMEM((tokens, rank), F32),
            pltpu.VMEM((tokens, rank), BF16),
            pltpu.VMEM((tokens, rank), BF16),
            dma((2,)), dma((n_dp,)), dma((n_dp,)), dma((n_dp,)), dma((4 + n_dp,)),
        ]
        + [dma((n_dp - 1,))] * 10
        + [dma((n_chunks, PIECES))] * 2,
        compiler_params=pltpu.CompilerParams(
            collective_id=0, has_side_effects=True, vmem_limit_bytes=60 * 1024 * 1024
        ),
        cost_estimate=pl.CostEstimate(flops=10 * tokens * depth * rank, bytes_accessed=20 * 2**20, transcendentals=0),
    )(rows, top, mean, hess, noise)


def update_kernel(
    in_scale, out_scale, n_dp,
    rows_t, inc_t, branch_t, hidden_t, mean_r, hess_r, mom_r, noise_r, next_r,
    mean_o, hess_o, mom_o, weights_o,
):
    contract = (((0,), (0,)), ((), ()))
    for i in range(2):
        total = None
        for d in range(n_dp):
            if i == 0:
                grad = lax.dot_general(rows_t[d], branch_t[d], contract, preferred_element_type=F32) * in_scale
            else:
                grad = lax.dot_general(inc_t[d], hidden_t[d], contract, preferred_element_type=F32) * out_scale
            grad = grad.astype(BF16).astype(F32)
            with_noise = grad * noise_r[d, i].astype(F32)
            if total is None:
                total, total_noise = grad, with_noise
            else:
                total, total_noise = total + grad, total_noise + with_noise
        own_hessian = hess_r[i]
        own_mean = mean_r[i]
        grad_mean = total * (1.0 / n_dp)
        hess_est = total_noise * (1.0 / n_dp) * jnp.sqrt(sample_size * (own_hessian + weight_decay))
        new_momentum = first_decay * mom_r[i] + (1.0 - first_decay) * grad_mean
        new_hessian = (
            second_decay * own_hessian
            + (1.0 - second_decay) * hess_est
            + 0.5 * (1.0 - second_decay) ** 2 * (own_hessian - hess_est) ** 2 / (own_hessian + weight_decay)
        )
        new_mean = own_mean - step_rate * (
            new_momentum / (1.0 - first_decay**step_number) + weight_decay * own_mean
        ) / (new_hessian + weight_decay)
        next_spread = 1.0 / jnp.sqrt(sample_size * (new_hessian + weight_decay))
        mean_o[i] = new_mean
        hess_o[i] = new_hessian
        mom_o[i] = new_momentum
        for d in range(n_dp):
            weights_o[d, i] = (new_mean + next_spread * next_r[d, i].astype(F32)).astype(BF16)


def update(n_dp, depth, rows_t, inc_t, branch_t, hidden_t, mean, hess, mom, noise, noise_next):
    _, tokens, width = rows_t.shape
    rank = mean.shape[-1]
    block = 256
    in_scale = 1.0 / math.sqrt(depth)
    out_scale = branch_gain / math.sqrt(rank)
    cols = pl.BlockSpec((n_dp, tokens, block), lambda r: (0, 0, r))
    small = pl.BlockSpec((n_dp, tokens, rank), lambda r: (0, 0, 0))
    state = pl.BlockSpec((2, block, rank), lambda r: (0, r, 0))
    wide = pl.BlockSpec((n_dp, 2, block, rank), lambda r: (0, 0, r, 0))
    shape = jax.ShapeDtypeStruct(mean.shape, F32)
    return pl.pallas_call(
        functools.partial(update_kernel, in_scale, out_scale, n_dp),
        grid=(width // block,),
        out_shape=(shape, shape, shape, jax.ShapeDtypeStruct(noise.shape, BF16)),
        in_specs=[cols, cols, small, small, state, state, state, wide, wide],
        out_specs=(state, state, state, wide),
        compiler_params=pltpu.CompilerParams(vmem_limit_bytes=60 * 1024 * 1024),
        cost_estimate=pl.CostEstimate(
            flops=4 * n_dp * tokens * width * rank, bytes_accessed=22 * 2**20, transcendentals=0
        ),
    )(rows_t, inc_t, branch_t, hidden_t, mean, hess, mom, noise, noise_next)


def on_device(n_sec, n_dp, layer_input, top_grad, mean, hessian, momentum, noise, noise_next):
    input_grad, rows_t, inc_t, branch_t, hidden_t = chain(
        n_sec, n_dp, layer_input[0], top_grad, mean[0], hessian[0], noise[0]
    )
    new_mean, new_hessian, new_momentum, next_weights = update(
        n_dp, layer_input.shape[-1], rows_t, inc_t, branch_t, hidden_t,
        mean[0], hessian[0], momentum[0], noise[0], noise_next[0],
    )
    return (input_grad[None], new_mean[None], new_hessian[None], new_momentum[None], next_weights[None])


def solution(mesh):
    in_specs = (
        P("section", "dp", None),
        P("dp", None),
        P("section", None, "dp", None),
        P("section", None, "dp", None),
        P("section", None, "dp", None),
        P("section", None, None, "dp", None),
        P("section", None, None, "dp", None),
    )
    out_specs = (
        P("section", "dp", None),
        P("section", None, "dp", None),
        P("section", None, "dp", None),
        P("section", None, "dp", None),
        P("section", None, None, "dp", None),
    )
    return jax.shard_map(
        functools.partial(on_device, mesh.shape["section"], mesh.shape["dp"]),
        mesh=mesh, in_specs=in_specs, out_specs=out_specs, check_vma=False,
    )
```

```python
import functools
import math

import jax
import jax.numpy as jnp
from jax import lax
from jax.experimental import pallas as pl
from jax.experimental.pallas import tpu as pltpu
from jax.sharding import PartitionSpec as P

MESH = pl.DeviceIdType.MESH
F32 = jnp.float32
BF16 = jnp.bfloat16

sample_size = 4.0
weight_decay = 0.05
first_decay = 0.9
second_decay = 0.9
step_rate = 0.5
branch_gain = 0.5
step_number = 10.0

CHUNK = 8
FOLD = 2 * CHUNK
PIECES = 2


def chain_kernel(
    n_sec, n_dp,
    rows_hbm, top_hbm, mean_hbm, hess_hbm, noise_hbm,
    ig_hbm, rows_t, inc_t, branch_t, hidden_t,
    mean_v, spread_v, noise_v, rows_v, inc_v, out_v, top_v, send_w, w_v, turned_w, preact_v, slope_v, hidden_f, hidden_v,
    branch_f, branch_v,
    state_sem, noise_sem, rows_sem, top_sem, local_sem,
    w_send, w_recv, rt_send, rt_recv, it_send, it_recv, h_send, h_recv, b_send, b_recv, c_send, c_recv,
):
    s = lax.axis_index("section")
    j = lax.axis_index("dp")
    last = n_sec - 1
    tokens = rows_v.shape[1]
    width = rows_v.shape[2]
    half = width // 2
    n_chunks = tokens // CHUNK
    per = n_dp // PIECES
    rank = branch_v.shape[1]
    in_scale = 1.0 / math.sqrt(width * n_dp)
    out_scale = branch_gain / math.sqrt(rank)

    def peer_of(k):
        return lax.rem(j + k, n_dp)

    def source_of(k):
        return lax.rem(j + n_dp - k, n_dp)

    def remote(src, dst, send, recv, **device):
        return pltpu.make_async_remote_copy(
            src_ref=src, dst_ref=dst, send_sem=send, recv_sem=recv, device_id=device, device_id_type=MESH
        )

    mean_in = pltpu.make_async_copy(mean_hbm, mean_v, state_sem.at[0])
    hess_in = pltpu.make_async_copy(hess_hbm, spread_v, state_sem.at[1])
    hess_in.start()
    mean_in.start()
    for k in range(1, n_dp + 1):
        pltpu.make_async_copy(noise_hbm.at[peer_of(k)], noise_v.at[k - 1], noise_sem.at[k - 1]).start()
    for b in range(n_dp):
        pltpu.make_async_copy(rows_hbm.at[:, pl.ds(b * width, width)], rows_v.at[b], rows_sem.at[b]).start()

    def top_copy(b):
        return pltpu.make_async_copy(top_hbm.at[:, pl.ds(b * width, width)], top_v.at[b], top_sem.at[b])

    @pl.when(s == last)
    def _():
        for b in range(n_dp):
            top_copy(b).start()

    barrier = pltpu.get_barrier_semaphore()
    for k in range(1, n_dp):
        pl.semaphore_signal(barrier, inc=1, device_id={"dp": peer_of(k)}, device_id_type=MESH)
    above = lax.rem(s + 1, n_sec)
    below = lax.rem(s + n_sec - 1, n_sec)
    pl.semaphore_signal(barrier, inc=1, device_id={"section": above}, device_id_type=MESH)
    pl.semaphore_signal(barrier, inc=1, device_id={"section": below}, device_id_type=MESH)

    hess_in.wait()
    mean_in.wait()
    step_rows = min(128, half)

    def each_rows(body):
        for i in range(2):
            for h in range(2):
                def turn(r, carry):
                    first = pl.multiple_of(r * step_rows, step_rows)
                    body(i, pl.ds(h * half + first, step_rows), pl.ds(first, step_rows), pl.ds(h * rank, rank))
                    return carry
                lax.fori_loop(0, half // step_rows, turn, 0)

    def make_spread(i, rr, folded, lanes):
        spread_v[i, rr, :] = 1.0 / jnp.sqrt(sample_size * (spread_v[i, rr, :] + weight_decay))

    each_rows(make_spread)
    pl.semaphore_wait(barrier, n_dp + 1)

    def weight_copy(k):
        return remote(send_w.at[k - 1], w_v.at[j], w_send.at[k - 1], w_recv.at[k - 1], dp=peer_of(k))

    def make_weights(k, carry):
        pltpu.make_async_copy(noise_hbm.at[peer_of(k)], noise_v.at[k - 1], noise_sem.at[k - 1]).wait()

        def body(i, rr, folded, lanes):
            send_w[k - 1, i, folded, lanes] = (
                mean_v[i, rr, :] + spread_v[i, rr, :] * noise_v[k - 1, i, rr, :].astype(F32)
            ).astype(BF16)

        each_rows(body)
        weight_copy(k).start()
        return carry

    lax.fori_loop(1, n_dp, make_weights, 0)
    pltpu.make_async_copy(noise_hbm.at[j], noise_v.at[n_dp - 1], noise_sem.at[n_dp - 1]).wait()

    def own_weights(i, rr, folded, lanes):
        w_v[j, i, folded, lanes] = (
            mean_v[i, rr, :] + spread_v[i, rr, :] * noise_v[n_dp - 1, i, rr, :].astype(F32)
        ).astype(BF16)

    each_rows(own_weights)
    for b in range(n_dp):
        pltpu.make_async_copy(rows_hbm.at[:, pl.ds(b * width, width)], rows_v.at[b], rows_sem.at[b]).wait()

    def block_preact(src):
        return jnp.dot(
            rows_v[src, :, :half], w_v[src, 0, :, :rank], preferred_element_type=F32
        ) + jnp.dot(rows_v[src, :, half:], w_v[src, 0, :, rank:], preferred_element_type=F32)

    def turn_block(src):
        turned_w[src] = w_v[src, 0].T

    preact_v[...] = block_preact(j)
    turn_block(j)

    def add_preact(k, carry):
        weight_copy(k).wait_recv()
        preact_v[...] += block_preact(source_of(k))
        turn_block(source_of(k))
        return carry

    lax.fori_loop(1, n_dp, add_preact, 0)
    preact = preact_v[...] * in_scale
    gate = jax.nn.sigmoid(preact)
    hidden_f[...] = preact * gate
    slope_v[...] = gate * (1.0 + preact * (1.0 - gate)) * out_scale
    for c in range(n_chunks):
        part = hidden_f[c * CHUNK : (c + 1) * CHUNK, :]
        hidden_v[c * FOLD : (c + 1) * FOLD, :] = jnp.concatenate([part, part], 0).astype(BF16)

    @pl.when(s == last)
    def _():
        for b in range(n_dp):
            top_copy(b).wait()

            def fold(q, carry):
                pair = top_v[b, pl.ds(pl.multiple_of(q * FOLD, FOLD), FOLD), :].astype(F32)
                for u in range(2):
                    part = pair[u * CHUNK : (u + 1) * CHUNK]
                    inc_v[b, pl.ds(pl.multiple_of((2 * q + u) * FOLD, FOLD), FOLD), :] = jnp.concatenate(
                        [part[:, :half], part[:, half:]], 0
                    ).astype(BF16)
                return carry

            lax.fori_loop(0, n_chunks // 2, fold, 0)

    def chain_copy(c, p):
        part = (pl.ds(p * per, per), pl.ds(pl.multiple_of(c * FOLD, FOLD), FOLD))
        return remote(out_v.at[part], inc_v.at[part], c_send.at[c, p], c_recv.at[c, p], section=below)

    def inc_copy(q, k):
        tok = pl.ds(pl.multiple_of(q * 2 * FOLD, 2 * FOLD), 2 * FOLD)
        return remote(inc_v.at[peer_of(k), tok], inc_t.at[j, tok], it_send.at[k - 1], it_recv.at[k - 1], dp=peer_of(k))

    def rows_copy(k):
        return remote(rows_v.at[peer_of(k)], rows_t.at[j], rt_send.at[k - 1], rt_recv.at[k - 1], dp=peer_of(k))

    def hidden_copy(k):
        return remote(hidden_v, hidden_t.at[j], h_send.at[k - 1], h_recv.at[k - 1], dp=peer_of(k))

    def branch_copy(k):
        return remote(branch_v, branch_t.at[j], b_send.at[k - 1], b_recv.at[k - 1], dp=peer_of(k))

    late = jnp.logical_and(s >= n_sec // 2, s < n_sec // 2 + 2)

    def send_inc(q):
        def turn(k, carry):
            inc_copy(q, k).start()
            return carry
        lax.fori_loop(1, n_dp, turn, 0)

    def one_chunk(c):
        tok = pl.ds(pl.multiple_of(c * CHUNK, CHUNK), CHUNK)
        folded = pl.ds(pl.multiple_of(c * FOLD, FOLD), FOLD)
        back = jnp.zeros((FOLD, 2 * rank), F32)
        for p in range(PIECES):
            @pl.when(s < last)
            def _():
                chain_copy(c, p).wait_recv()
            for b in range(p * per, (p + 1) * per):
                back += jnp.dot(inc_v[b, folded, :], w_v[b, 1], preferred_element_type=F32)
        branch = (back[:CHUNK, :rank] + back[CHUNK:, rank:]) * slope_v[tok, :]
        branch_f[tok, :] = branch
        nothing = jnp.zeros_like(branch)
        spread_branch = jnp.concatenate(
            [jnp.concatenate([branch, nothing], 1), jnp.concatenate([nothing, branch], 1)], 0
        ).astype(BF16)
        for p in range(PIECES):
            for b in range(p * per, (p + 1) * per):
                through = jnp.dot(spread_branch, turned_w[b], preferred_element_type=F32)
                out_v[b, folded, :] = (inc_v[b, folded, :].astype(F32) + through * in_scale).astype(BF16)

            @pl.when(s > 0)
            def _():
                chain_copy(c, p).start()

    def pair_turn(q, carry):
        one_chunk(2 * q)
        one_chunk(2 * q + 1)

        @pl.when(jnp.logical_not(late))
        def _():
            send_inc(q)

        return carry

    def send_rows(k, carry):
        rows_copy(k).start()
        hidden_copy(k).start()
        return carry

    lax.fori_loop(1, n_dp, send_rows, 0)
    lax.fori_loop(0, n_chunks // 2, pair_turn, 0)
    branch_v[...] = branch_f[...].astype(BF16)

    @pl.when(late)
    def _():
        def send_late(q, carry):
            send_inc(q)
            return carry
        lax.fori_loop(0, n_chunks // 2, send_late, 0)

    own = [
        pltpu.make_async_copy(branch_v, branch_t.at[j], local_sem.at[0]),
        pltpu.make_async_copy(hidden_v, hidden_t.at[j], local_sem.at[1]),
        pltpu.make_async_copy(rows_v.at[j], rows_t.at[j], local_sem.at[2]),
        pltpu.make_async_copy(inc_v.at[j], inc_t.at[j], local_sem.at[3]),
        pltpu.make_async_copy(out_v, ig_hbm, local_sem.at[4]),
    ]
    def send_branch(k, carry):
        branch_copy(k).start()
        return carry
    lax.fori_loop(1, n_dp, send_branch, 0)
    for copy in own:
        copy.start()

    def finish(k, carry):
        weight_copy(k).wait_send()
        rows_copy(k).wait()
        hidden_copy(k).wait()
        branch_copy(k).wait()
        whole = remote(inc_v.at[peer_of(k)], inc_t.at[j], it_send.at[k - 1], it_recv.at[k - 1], dp=peer_of(k))
        whole.wait()
        return carry

    lax.fori_loop(1, n_dp, finish, 0)

    @pl.when(s > 0)
    def _():
        def sent(c, carry):
            for p in range(PIECES):
                chain_copy(c, p).wait_send()
            return carry
        lax.fori_loop(0, n_chunks, sent, 0)

    for copy in own:
        copy.wait()


def chain(n_sec, n_dp, rows, top, mean, hess, noise):
    tokens, depth = rows.shape
    width = depth // n_dp
    rank = mean.shape[-1]
    n_chunks = tokens // CHUNK
    half = width // 2
    dma = pltpu.SemaphoreType.DMA
    hbm = pl.BlockSpec(memory_space=pltpu.HBM)
    return pl.pallas_call(
        functools.partial(chain_kernel, n_sec, n_dp),
        out_shape=(
            jax.ShapeDtypeStruct((n_dp, 2 * tokens, half), BF16),
            jax.ShapeDtypeStruct((n_dp, tokens, width), BF16),
            jax.ShapeDtypeStruct((n_dp, 2 * tokens, half), BF16),
            jax.ShapeDtypeStruct((n_dp, tokens, rank), BF16),
            jax.ShapeDtypeStruct((n_dp, 2 * tokens, rank), BF16),
        ),
        in_specs=[hbm] * 5,
        out_specs=(hbm,) * 5,
        scratch_shapes=[
            pltpu.VMEM((2, width, rank), F32),
            pltpu.VMEM((2, width, rank), F32),
            pltpu.VMEM((n_dp, 2, width, rank), BF16),
            pltpu.VMEM((n_dp, tokens, width), BF16),
            pltpu.VMEM((n_dp, 2 * tokens, half), BF16),
            pltpu.VMEM((n_dp, 2 * tokens, half), BF16),
            pltpu.VMEM((n_dp, tokens, width), BF16),
            pltpu.VMEM((n_dp - 1, 2, half, 2 * rank), BF16),
            pltpu.VMEM((n_dp, 2, half, 2 * rank), BF16),
            pltpu.VMEM((n_dp, 2 * rank, half), BF16),
            pltpu.VMEM((tokens, rank), F32),
            pltpu.VMEM((tokens, rank), F32),
            pltpu.VMEM((tokens, rank), F32),
            pltpu.VMEM((2 * tokens, rank), BF16),
            pltpu.VMEM((tokens, rank), F32),
            pltpu.VMEM((tokens, rank), BF16),
            dma((2,)), dma((n_dp,)), dma((n_dp,)), dma((n_dp,)), dma((5,)),
        ]
        + [dma((n_dp - 1,))] * 10
        + [dma((n_chunks, PIECES))] * 2,
        compiler_params=pltpu.CompilerParams(
            collective_id=0, has_side_effects=True, vmem_limit_bytes=27 * 1024 * 1024
        ),
        cost_estimate=pl.CostEstimate(flops=10 * tokens * depth * rank, bytes_accessed=20 * 2**20, transcendentals=0),
    )(*(pltpu.with_memory_space_constraint(x, pltpu.HBM) for x in (rows, top, mean, hess, noise)))


def update_kernel(
    in_scale, out_scale, n_dp,
    ig_hbm, rows_hbm, inc_hbm, branch_t, hidden_t, mean_r, hess_r, mom_r, noise_r, next_r,
    ig_o, mean_o, hess_o, mom_o, weights_o,
    ig_v, rows_v, inc_v, ig_sem, rows_sem, inc_sem,
):
    turn = pl.program_id(0)
    steps, block = rows_v.shape[0], rows_v.shape[3]
    half_steps, fold_rows = inc_v.shape[0], ig_v.shape[2]

    def ig_copy(r):
        return pltpu.make_async_copy(
            ig_hbm.at[:, pl.ds(pl.multiple_of(r * fold_rows, fold_rows), fold_rows)], ig_v.at[r], ig_sem.at[r]
        )

    def rows_copy(r):
        return pltpu.make_async_copy(
            rows_hbm.at[:, :, pl.ds(pl.multiple_of(r * block, block), block)], rows_v.at[r], rows_sem.at[r]
        )

    def inc_copy(r):
        return pltpu.make_async_copy(
            inc_hbm.at[:, :, pl.ds(pl.multiple_of(r * block, block), block)], inc_v.at[r], inc_sem.at[r]
        )

    @pl.when(turn == 0)
    def _():
        for r in range(steps):
            rows_copy(r).start()
            if r < half_steps:
                inc_copy(r).start()
            ig_copy(r).start()

    @pl.when(turn < half_steps)
    def _():
        inc_copy(turn).wait()

    rows_copy(turn).wait()
    ig_copy(turn).wait()
    ig_fold, rows_t, inc_t = ig_v.at[turn], rows_v.at[turn], inc_v.at[lax.rem(turn, half_steps)]
    contract = (((0,), (0,)), ((), ()))
    width = 2 * ig_fold.shape[2]
    for b in range(n_dp):
        for q in range(ig_fold.shape[1] // (2 * FOLD)):
            natural = []
            for u in range(2):
                part = ig_fold[b, (2 * q + u) * FOLD : (2 * q + u + 1) * FOLD, :].astype(F32)
                natural.append(jnp.concatenate([part[:CHUNK], part[CHUNK:]], 1))
            ig_o[q * FOLD : (q + 1) * FOLD, b * width : (b + 1) * width] = jnp.concatenate(natural, 0).astype(BF16)
    which = pl.program_id(0) // (pl.num_programs(0) // 2)
    row = lax.broadcasted_iota(jnp.int32, hidden_t.shape[1:], 0)
    own_half = lax.rem(row // CHUNK, 2) == which
    for i in range(2):
        total = None
        for d in range(n_dp):
            if i == 0:
                grad = lax.dot_general(rows_t[d], branch_t[d], contract, preferred_element_type=F32) * in_scale
            else:
                grad = lax.dot_general(inc_t[d], jnp.where(own_half, hidden_t[d], jnp.zeros_like(hidden_t[d])), contract, preferred_element_type=F32) * out_scale
            grad = grad.astype(BF16).astype(F32)
            with_noise = grad * noise_r[d, i].astype(F32)
            if total is None:
                total, total_noise = grad, with_noise
            else:
                total, total_noise = total + grad, total_noise + with_noise
        own_hessian = hess_r[i]
        own_mean = mean_r[i]
        grad_mean = total * (1.0 / n_dp)
        hess_est = total_noise * (1.0 / n_dp) * jnp.sqrt(sample_size * (own_hessian + weight_decay))
        new_momentum = first_decay * mom_r[i] + (1.0 - first_decay) * grad_mean
        new_hessian = (
            second_decay * own_hessian
            + (1.0 - second_decay) * hess_est
            + 0.5 * (1.0 - second_decay) ** 2 * (own_hessian - hess_est) ** 2 / (own_hessian + weight_decay)
        )
        new_mean = own_mean - step_rate * (
            new_momentum / (1.0 - first_decay**step_number) + weight_decay * own_mean
        ) / (new_hessian + weight_decay)
        next_spread = 1.0 / jnp.sqrt(sample_size * (new_hessian + weight_decay))
        mean_o[i] = new_mean
        hess_o[i] = new_hessian
        mom_o[i] = new_momentum
        for d in range(n_dp):
            weights_o[d, i] = (new_mean + next_spread * next_r[d, i].astype(F32)).astype(BF16)


def update(n_dp, depth, ig_fold, rows_t, inc_t, branch_t, hidden_t, mean, hess, mom, noise, noise_next):
    _, tokens, width = rows_t.shape
    rank = mean.shape[-1]
    block = min(256, width // 2)
    steps = width // block
    half_steps = steps // 2
    in_scale = 1.0 / math.sqrt(depth)
    out_scale = branch_gain / math.sqrt(rank)
    hbm = pl.BlockSpec(memory_space=pltpu.HBM)
    grads_out = pl.BlockSpec((tokens // steps, depth), lambda r: (r, 0))
    small = pl.BlockSpec((n_dp, tokens, rank), lambda r: (0, 0, 0))
    small2 = pl.BlockSpec((n_dp, 2 * tokens, rank), lambda r: (0, 0, 0))
    state = pl.BlockSpec((2, block, rank), lambda r: (0, r, 0))
    wide = pl.BlockSpec((n_dp, 2, block, rank), lambda r: (0, 0, r, 0))
    shape = jax.ShapeDtypeStruct(mean.shape, F32)
    return pl.pallas_call(
        functools.partial(update_kernel, in_scale, out_scale, n_dp),
        grid=(steps,),
        out_shape=(jax.ShapeDtypeStruct((tokens, depth), BF16), shape, shape, shape, jax.ShapeDtypeStruct(noise.shape, BF16)),
        in_specs=[hbm, hbm, hbm, small, small2, state, state, state, wide, wide],
        out_specs=(grads_out, state, state, state, wide),
        scratch_shapes=[
            pltpu.VMEM((steps, n_dp, 2 * tokens // steps, width // 2), BF16),
            pltpu.VMEM((steps, n_dp, tokens, block), BF16),
            pltpu.VMEM((half_steps, n_dp, 2 * tokens, block), BF16),
            pltpu.SemaphoreType.DMA((steps,)), pltpu.SemaphoreType.DMA((steps,)), pltpu.SemaphoreType.DMA((half_steps,)),
        ],
        compiler_params=pltpu.CompilerParams(vmem_limit_bytes=34 * 1024 * 1024),
        cost_estimate=pl.CostEstimate(
            flops=4 * n_dp * tokens * width * rank, bytes_accessed=22 * 2**20, transcendentals=0
        ),
    )(
        ig_fold, rows_t, inc_t, branch_t, hidden_t, mean, hess,
        pltpu.with_memory_space_constraint(mom, pltpu.HBM), noise, noise_next,
    )


def on_device(n_sec, n_dp, layer_input, top_grad, mean, hessian, momentum, noise, noise_next):
    ig_fold, rows_t, inc_t, branch_t, hidden_t = chain(
        n_sec, n_dp, layer_input[0], top_grad, mean[0], hessian[0], noise[0]
    )
    input_grad, new_mean, new_hessian, new_momentum, next_weights = update(
        n_dp, layer_input.shape[-1], ig_fold, rows_t, inc_t, branch_t, hidden_t,
        mean[0], hessian[0], momentum[0], noise[0], noise_next[0],
    )
    return (input_grad[None], new_mean[None], new_hessian[None], new_momentum[None], next_weights[None])


def solution(mesh):
    in_specs = (
        P("section", "dp", None),
        P("dp", None),
        P("section", None, "dp", None),
        P("section", None, "dp", None),
        P("section", None, "dp", None),
        P("section", None, None, "dp", None),
        P("section", None, None, "dp", None),
    )
    out_specs = (
        P("section", "dp", None),
        P("section", None, "dp", None),
        P("section", None, "dp", None),
        P("section", None, "dp", None),
        P("section", None, None, "dp", None),
    )
    return jax.shard_map(
        functools.partial(on_device, mesh.shape["section"], mesh.shape["dp"]),
        mesh=mesh, in_specs=in_specs, out_specs=out_specs, check_vma=False,
    )
```

```python
import functools
import math

import jax
import jax.numpy as jnp
from jax import lax
from jax.experimental import pallas as pl
from jax.experimental.pallas import tpu as pltpu
from jax.sharding import PartitionSpec as P

MESH = pl.DeviceIdType.MESH
F32 = jnp.float32
BF16 = jnp.bfloat16

sample_size = 4.0
weight_decay = 0.05
first_decay = 0.9
second_decay = 0.9
step_rate = 0.5
branch_gain = 0.5
step_number = 10.0

CHUNK = 8
FOLD = 2 * CHUNK
PIECES = 3


def chain_kernel(
    n_sec, n_dp,
    rows_hbm, top_hbm, mean_hbm, hess_hbm, noise_hbm,
    ig_hbm, rows_t, inc_t, branch_t, hidden_t,
    mean_v, spread_v, noise_v, rows_v, inc_v, out_v, top_v, send_w, w_v, turned_w, preact_v, slope_v, hidden_f, hidden_v,
    branch_f, branch_v,
    state_sem, noise_sem, rows_sem, top_sem, local_sem,
    w_send, w_recv, rt_send, rt_recv, it_send, it_recv, h_send, h_recv, b_send, b_recv, c_send, c_recv,
):
    s = lax.axis_index("section")
    j = lax.axis_index("dp")
    last = n_sec - 1
    tokens = rows_v.shape[1]
    width = rows_v.shape[2]
    half = width // 2
    n_chunks = tokens // CHUNK
    bounds = (0, n_dp // 4, 3 * n_dp // 4, n_dp)
    rank = branch_v.shape[1]
    in_scale = 1.0 / math.sqrt(width * n_dp)
    out_scale = branch_gain / math.sqrt(rank)

    def peer_of(k):
        return lax.rem(j + k, n_dp)

    def source_of(k):
        return lax.rem(j + n_dp - k, n_dp)

    def remote(src, dst, send, recv, **device):
        return pltpu.make_async_remote_copy(
            src_ref=src, dst_ref=dst, send_sem=send, recv_sem=recv, device_id=device, device_id_type=MESH
        )

    mean_in = pltpu.make_async_copy(mean_hbm, mean_v, state_sem.at[0])
    hess_in = pltpu.make_async_copy(hess_hbm, spread_v, state_sem.at[1])
    hess_in.start()
    mean_in.start()
    for k in range(1, n_dp + 1):
        pltpu.make_async_copy(noise_hbm.at[peer_of(k)], noise_v.at[k - 1], noise_sem.at[k - 1]).start()
    for b in range(n_dp):
        pltpu.make_async_copy(rows_hbm.at[:, pl.ds(b * width, width)], rows_v.at[b], rows_sem.at[b]).start()

    def top_copy(b):
        return pltpu.make_async_copy(top_hbm.at[:, pl.ds(b * width, width)], top_v.at[b], top_sem.at[b])

    @pl.when(s == last)
    def _():
        for b in range(n_dp):
            top_copy(b).start()

    barrier = pltpu.get_barrier_semaphore()
    for k in range(1, n_dp):
        pl.semaphore_signal(barrier, inc=1, device_id={"dp": peer_of(k)}, device_id_type=MESH)
    above = lax.rem(s + 1, n_sec)
    below = lax.rem(s + n_sec - 1, n_sec)
    pl.semaphore_signal(barrier, inc=1, device_id={"section": above}, device_id_type=MESH)
    pl.semaphore_signal(barrier, inc=1, device_id={"section": below}, device_id_type=MESH)

    hess_in.wait()
    mean_in.wait()
    step_rows = min(128, half)

    def each_rows(body):
        for i in range(2):
            for h in range(2):
                def turn(r, carry):
                    first = pl.multiple_of(r * step_rows, step_rows)
                    body(i, pl.ds(h * half + first, step_rows), pl.ds(first, step_rows), pl.ds(h * rank, rank))
                    return carry
                lax.fori_loop(0, half // step_rows, turn, 0)

    def make_spread(i, rr, folded, lanes):
        spread_v[i, rr, :] = 1.0 / jnp.sqrt(sample_size * (spread_v[i, rr, :] + weight_decay))

    each_rows(make_spread)
    pl.semaphore_wait(barrier, n_dp + 1)

    def weight_copy(k):
        return remote(send_w.at[k - 1], w_v.at[j], w_send.at[k - 1], w_recv.at[k - 1], dp=peer_of(k))

    def make_weights(k, carry):
        pltpu.make_async_copy(noise_hbm.at[peer_of(k)], noise_v.at[k - 1], noise_sem.at[k - 1]).wait()

        def body(i, rr, folded, lanes):
            send_w[k - 1, i, folded, lanes] = (
                mean_v[i, rr, :] + spread_v[i, rr, :] * noise_v[k - 1, i, rr, :].astype(F32)
            ).astype(BF16)

        each_rows(body)
        weight_copy(k).start()
        return carry

    lax.fori_loop(1, n_dp, make_weights, 0)
    pltpu.make_async_copy(noise_hbm.at[j], noise_v.at[n_dp - 1], noise_sem.at[n_dp - 1]).wait()

    def own_weights(i, rr, folded, lanes):
        w_v[j, i, folded, lanes] = (
            mean_v[i, rr, :] + spread_v[i, rr, :] * noise_v[n_dp - 1, i, rr, :].astype(F32)
        ).astype(BF16)

    each_rows(own_weights)
    for b in range(n_dp):
        pltpu.make_async_copy(rows_hbm.at[:, pl.ds(b * width, width)], rows_v.at[b], rows_sem.at[b]).wait()

    def block_preact(src):
        return jnp.dot(
            rows_v[src, :, :half], w_v[src, 0, :, :rank], preferred_element_type=F32
        ) + jnp.dot(rows_v[src, :, half:], w_v[src, 0, :, rank:], preferred_element_type=F32)

    def turn_block(src):
        turned_w[src] = w_v[src, 0].T

    preact_v[...] = block_preact(j)
    turn_block(j)

    def add_preact(k, carry):
        weight_copy(k).wait_recv()
        preact_v[...] += block_preact(source_of(k))
        turn_block(source_of(k))
        return carry

    lax.fori_loop(1, n_dp, add_preact, 0)
    preact = preact_v[...] * in_scale
    gate = jax.nn.sigmoid(preact)
    hidden_f[...] = preact * gate
    slope_v[...] = gate * (1.0 + preact * (1.0 - gate)) * out_scale
    for c in range(n_chunks):
        part = hidden_f[c * CHUNK : (c + 1) * CHUNK, :]
        hidden_v[c * FOLD : (c + 1) * FOLD, :] = jnp.concatenate([part, part], 0).astype(BF16)

    @pl.when(s == last)
    def _():
        for b in range(n_dp):
            top_copy(b).wait()

            def fold(q, carry):
                pair = top_v[b, pl.ds(pl.multiple_of(q * FOLD, FOLD), FOLD), :].astype(F32)
                for u in range(2):
                    part = pair[u * CHUNK : (u + 1) * CHUNK]
                    inc_v[b, pl.ds(pl.multiple_of((2 * q + u) * FOLD, FOLD), FOLD), :] = jnp.concatenate(
                        [part[:, :half], part[:, half:]], 0
                    ).astype(BF16)
                return carry

            lax.fori_loop(0, n_chunks // 2, fold, 0)

    def chain_copy(c, p):
        part = (pl.ds(bounds[p], bounds[p + 1] - bounds[p]), pl.ds(pl.multiple_of(c * FOLD, FOLD), FOLD))
        return remote(out_v.at[part], inc_v.at[part], c_send.at[c, p], c_recv.at[c, p], section=below)

    def inc_copy(q, k):
        tok = pl.ds(pl.multiple_of(q * 2 * FOLD, 2 * FOLD), 2 * FOLD)
        return remote(inc_v.at[peer_of(k), tok], inc_t.at[j, tok], it_send.at[k - 1], it_recv.at[k - 1], dp=peer_of(k))

    def rows_copy(k):
        return remote(rows_v.at[peer_of(k)], rows_t.at[j], rt_send.at[k - 1], rt_recv.at[k - 1], dp=peer_of(k))

    def hidden_copy(k):
        return remote(hidden_v, hidden_t.at[j], h_send.at[k - 1], h_recv.at[k - 1], dp=peer_of(k))

    def branch_copy(k):
        return remote(branch_v, branch_t.at[j], b_send.at[k - 1], b_recv.at[k - 1], dp=peer_of(k))

    late = jnp.logical_and(s >= n_sec // 2, s < n_sec // 2 + 2)

    def send_inc(q):
        def turn(k, carry):
            inc_copy(q, k).start()
            return carry
        lax.fori_loop(1, n_dp, turn, 0)

    def one_chunk(c):
        tok = pl.ds(pl.multiple_of(c * CHUNK, CHUNK), CHUNK)
        folded = pl.ds(pl.multiple_of(c * FOLD, FOLD), FOLD)
        back = jnp.zeros((FOLD, 2 * rank), F32)
        for p in range(PIECES):
            @pl.when(s < last)
            def _():
                chain_copy(c, p).wait_recv()
            for b in range(bounds[p], bounds[p + 1]):
                back += jnp.dot(inc_v[b, folded, :], w_v[b, 1], preferred_element_type=F32)
        branch = (back[:CHUNK, :rank] + back[CHUNK:, rank:]) * slope_v[tok, :]
        branch_f[tok, :] = branch
        nothing = jnp.zeros_like(branch)
        spread_branch = jnp.concatenate(
            [jnp.concatenate([branch, nothing], 1), jnp.concatenate([nothing, branch], 1)], 0
        ).astype(BF16)
        for p in range(PIECES):
            for b in range(bounds[p], bounds[p + 1]):
                through = jnp.dot(spread_branch, turned_w[b], preferred_element_type=F32)
                out_v[b, folded, :] = (inc_v[b, folded, :].astype(F32) + through * in_scale).astype(BF16)

            @pl.when(s > 0)
            def _():
                chain_copy(c, p).start()

    def pair_turn(q, carry):
        one_chunk(2 * q)
        one_chunk(2 * q + 1)

        @pl.when(jnp.logical_not(late))
        def _():
            send_inc(q)

        return carry

    def send_rows(k, carry):
        rows_copy(k).start()
        hidden_copy(k).start()
        return carry

    lax.fori_loop(1, n_dp, send_rows, 0)
    lax.fori_loop(0, n_chunks // 2, pair_turn, 0)
    branch_v[...] = branch_f[...].astype(BF16)

    @pl.when(late)
    def _():
        def send_late(q, carry):
            send_inc(q)
            return carry
        lax.fori_loop(0, n_chunks // 2, send_late, 0)

    own = [
        pltpu.make_async_copy(branch_v, branch_t.at[j], local_sem.at[0]),
        pltpu.make_async_copy(hidden_v, hidden_t.at[j], local_sem.at[1]),
        pltpu.make_async_copy(rows_v.at[j], rows_t.at[j], local_sem.at[2]),
        pltpu.make_async_copy(inc_v.at[j], inc_t.at[j], local_sem.at[3]),
        pltpu.make_async_copy(out_v, ig_hbm, local_sem.at[4]),
    ]
    def send_branch(k, carry):
        branch_copy(k).start()
        return carry
    lax.fori_loop(1, n_dp, send_branch, 0)
    for copy in own:
        copy.start()

    def finish(k, carry):
        weight_copy(k).wait_send()
        rows_copy(k).wait()
        hidden_copy(k).wait()
        branch_copy(k).wait()
        whole = remote(inc_v.at[peer_of(k)], inc_t.at[j], it_send.at[k - 1], it_recv.at[k - 1], dp=peer_of(k))
        whole.wait()
        return carry

    lax.fori_loop(1, n_dp, finish, 0)

    @pl.when(s > 0)
    def _():
        def sent(c, carry):
            for p in range(PIECES):
                chain_copy(c, p).wait_send()
            return carry
        lax.fori_loop(0, n_chunks, sent, 0)

    for copy in own:
        copy.wait()


def chain(n_sec, n_dp, rows, top, mean, hess, noise):
    tokens, depth = rows.shape
    width = depth // n_dp
    rank = mean.shape[-1]
    n_chunks = tokens // CHUNK
    half = width // 2
    dma = pltpu.SemaphoreType.DMA
    hbm = pl.BlockSpec(memory_space=pltpu.HBM)
    return pl.pallas_call(
        functools.partial(chain_kernel, n_sec, n_dp),
        out_shape=(
            jax.ShapeDtypeStruct((n_dp, 2 * tokens, half), BF16),
            jax.ShapeDtypeStruct((n_dp, tokens, width), BF16),
            jax.ShapeDtypeStruct((n_dp, 2 * tokens, half), BF16),
            jax.ShapeDtypeStruct((n_dp, tokens, rank), BF16),
            jax.ShapeDtypeStruct((n_dp, 2 * tokens, rank), BF16),
        ),
        in_specs=[hbm] * 5,
        out_specs=(hbm,) * 5,
        scratch_shapes=[
            pltpu.VMEM((2, width, rank), F32),
            pltpu.VMEM((2, width, rank), F32),
            pltpu.VMEM((n_dp, 2, width, rank), BF16),
            pltpu.VMEM((n_dp, tokens, width), BF16),
            pltpu.VMEM((n_dp, 2 * tokens, half), BF16),
            pltpu.VMEM((n_dp, 2 * tokens, half), BF16),
            pltpu.VMEM((n_dp, tokens, width), BF16),
            pltpu.VMEM((n_dp - 1, 2, half, 2 * rank), BF16),
            pltpu.VMEM((n_dp, 2, half, 2 * rank), BF16),
            pltpu.VMEM((n_dp, 2 * rank, half), BF16),
            pltpu.VMEM((tokens, rank), F32),
            pltpu.VMEM((tokens, rank), F32),
            pltpu.VMEM((tokens, rank), F32),
            pltpu.VMEM((2 * tokens, rank), BF16),
            pltpu.VMEM((tokens, rank), F32),
            pltpu.VMEM((tokens, rank), BF16),
            dma((2,)), dma((n_dp,)), dma((n_dp,)), dma((n_dp,)), dma((5,)),
        ]
        + [dma((n_dp - 1,))] * 10
        + [dma((n_chunks, PIECES))] * 2,
        compiler_params=pltpu.CompilerParams(
            collective_id=0, has_side_effects=True, vmem_limit_bytes=27 * 1024 * 1024
        ),
        cost_estimate=pl.CostEstimate(flops=10 * tokens * depth * rank, bytes_accessed=20 * 2**20, transcendentals=0),
    )(*(pltpu.with_memory_space_constraint(x, pltpu.HBM) for x in (rows, top, mean, hess, noise)))


def update_kernel(
    in_scale, out_scale, n_dp,
    ig_hbm, rows_hbm, inc_hbm, branch_t, hidden_t, mean_r, hess_r, mom_r, noise_r, next_r,
    ig_o, mean_o, hess_o, mom_o, weights_o,
    ig_v, rows_v, inc_v, ig_sem, rows_sem, inc_sem,
):
    turn = pl.program_id(0)
    steps, block = rows_v.shape[0], rows_v.shape[3]
    half_steps, fold_rows = inc_v.shape[0], ig_v.shape[2]

    def ig_copy(r):
        return pltpu.make_async_copy(
            ig_hbm.at[:, pl.ds(pl.multiple_of(r * fold_rows, fold_rows), fold_rows)], ig_v.at[r], ig_sem.at[r]
        )

    def rows_copy(r):
        return pltpu.make_async_copy(
            rows_hbm.at[:, :, pl.ds(pl.multiple_of(r * block, block), block)], rows_v.at[r], rows_sem.at[r]
        )

    def inc_copy(r):
        return pltpu.make_async_copy(
            inc_hbm.at[:, :, pl.ds(pl.multiple_of(r * block, block), block)], inc_v.at[r], inc_sem.at[r]
        )

    @pl.when(turn == 0)
    def _():
        for r in range(steps):
            rows_copy(r).start()
            if r < half_steps:
                inc_copy(r).start()
            ig_copy(r).start()

    @pl.when(turn < half_steps)
    def _():
        inc_copy(turn).wait()

    rows_copy(turn).wait()
    ig_copy(turn).wait()
    ig_fold, rows_t, inc_t = ig_v.at[turn], rows_v.at[turn], inc_v.at[lax.rem(turn, half_steps)]
    contract = (((0,), (0,)), ((), ()))
    width = 2 * ig_fold.shape[2]
    for b in range(n_dp):
        for q in range(ig_fold.shape[1] // (2 * FOLD)):
            natural = []
            for u in range(2):
                part = ig_fold[b, (2 * q + u) * FOLD : (2 * q + u + 1) * FOLD, :].astype(F32)
                natural.append(jnp.concatenate([part[:CHUNK], part[CHUNK:]], 1))
            ig_o[q * FOLD : (q + 1) * FOLD, b * width : (b + 1) * width] = jnp.concatenate(natural, 0).astype(BF16)
    which = pl.program_id(0) // (pl.num_programs(0) // 2)
    row = lax.broadcasted_iota(jnp.int32, hidden_t.shape[1:], 0)
    own_half = lax.rem(row // CHUNK, 2) == which
    for i in range(2):
        total = None
        for d in range(n_dp):
            if i == 0:
                grad = lax.dot_general(rows_t[d], branch_t[d], contract, preferred_element_type=F32) * in_scale
            else:
                grad = lax.dot_general(inc_t[d], jnp.where(own_half, hidden_t[d], jnp.zeros_like(hidden_t[d])), contract, preferred_element_type=F32) * out_scale
            grad = grad.astype(BF16).astype(F32)
            with_noise = grad * noise_r[d, i].astype(F32)
            if total is None:
                total, total_noise = grad, with_noise
            else:
                total, total_noise = total + grad, total_noise + with_noise
        own_hessian = hess_r[i]
        own_mean = mean_r[i]
        grad_mean = total * (1.0 / n_dp)
        hess_est = total_noise * (1.0 / n_dp) * jnp.sqrt(sample_size * (own_hessian + weight_decay))
        new_momentum = first_decay * mom_r[i] + (1.0 - first_decay) * grad_mean
        new_hessian = (
            second_decay * own_hessian
            + (1.0 - second_decay) * hess_est
            + 0.5 * (1.0 - second_decay) ** 2 * (own_hessian - hess_est) ** 2 / (own_hessian + weight_decay)
        )
        new_mean = own_mean - step_rate * (
            new_momentum / (1.0 - first_decay**step_number) + weight_decay * own_mean
        ) / (new_hessian + weight_decay)
        next_spread = 1.0 / jnp.sqrt(sample_size * (new_hessian + weight_decay))
        mean_o[i] = new_mean
        hess_o[i] = new_hessian
        mom_o[i] = new_momentum
        for d in range(n_dp):
            weights_o[d, i] = (new_mean + next_spread * next_r[d, i].astype(F32)).astype(BF16)


def update(n_dp, depth, ig_fold, rows_t, inc_t, branch_t, hidden_t, mean, hess, mom, noise, noise_next):
    _, tokens, width = rows_t.shape
    rank = mean.shape[-1]
    block = min(256, width // 2)
    steps = width // block
    half_steps = steps // 2
    in_scale = 1.0 / math.sqrt(depth)
    out_scale = branch_gain / math.sqrt(rank)
    hbm = pl.BlockSpec(memory_space=pltpu.HBM)
    grads_out = pl.BlockSpec((tokens // steps, depth), lambda r: (r, 0))
    small = pl.BlockSpec((n_dp, tokens, rank), lambda r: (0, 0, 0))
    small2 = pl.BlockSpec((n_dp, 2 * tokens, rank), lambda r: (0, 0, 0))
    state = pl.BlockSpec((2, block, rank), lambda r: (0, r, 0))
    wide = pl.BlockSpec((n_dp, 2, block, rank), lambda r: (0, 0, r, 0))
    shape = jax.ShapeDtypeStruct(mean.shape, F32)
    return pl.pallas_call(
        functools.partial(update_kernel, in_scale, out_scale, n_dp),
        grid=(steps,),
        out_shape=(jax.ShapeDtypeStruct((tokens, depth), BF16), shape, shape, shape, jax.ShapeDtypeStruct(noise.shape, BF16)),
        in_specs=[hbm, hbm, hbm, small, small2, state, state, state, wide, wide],
        out_specs=(grads_out, state, state, state, wide),
        scratch_shapes=[
            pltpu.VMEM((steps, n_dp, 2 * tokens // steps, width // 2), BF16),
            pltpu.VMEM((steps, n_dp, tokens, block), BF16),
            pltpu.VMEM((half_steps, n_dp, 2 * tokens, block), BF16),
            pltpu.SemaphoreType.DMA((steps,)), pltpu.SemaphoreType.DMA((steps,)), pltpu.SemaphoreType.DMA((half_steps,)),
        ],
        compiler_params=pltpu.CompilerParams(vmem_limit_bytes=34 * 1024 * 1024),
        cost_estimate=pl.CostEstimate(
            flops=4 * n_dp * tokens * width * rank, bytes_accessed=22 * 2**20, transcendentals=0
        ),
    )(
        ig_fold, rows_t, inc_t, branch_t, hidden_t, mean, hess,
        pltpu.with_memory_space_constraint(mom, pltpu.HBM), noise, noise_next,
    )


def on_device(n_sec, n_dp, layer_input, top_grad, mean, hessian, momentum, noise, noise_next):
    ig_fold, rows_t, inc_t, branch_t, hidden_t = chain(
        n_sec, n_dp, layer_input[0], top_grad, mean[0], hessian[0], noise[0]
    )
    input_grad, new_mean, new_hessian, new_momentum, next_weights = update(
        n_dp, layer_input.shape[-1], ig_fold, rows_t, inc_t, branch_t, hidden_t,
        mean[0], hessian[0], momentum[0], noise[0], noise_next[0],
    )
    return (input_grad[None], new_mean[None], new_hessian[None], new_momentum[None], next_weights[None])


def solution(mesh):
    in_specs = (
        P("section", "dp", None),
        P("dp", None),
        P("section", None, "dp", None),
        P("section", None, "dp", None),
        P("section", None, "dp", None),
        P("section", None, None, "dp", None),
        P("section", None, None, "dp", None),
    )
    out_specs = (
        P("section", "dp", None),
        P("section", None, "dp", None),
        P("section", None, "dp", None),
        P("section", None, "dp", None),
        P("section", None, None, "dp", None),
    )
    return jax.shard_map(
        functools.partial(on_device, mesh.shape["section"], mesh.shape["dp"]),
        mesh=mesh, in_specs=in_specs, out_specs=out_specs, check_vma=False,
    )
```
